128 devices in a mesh: layer: 16 (over z, x), tok: 8 (over y, core).
Axes of the slice: x: 4, y: 4, z: 4, core: 2. Of those that a mesh axis runs over, the one named last changes fastest.
Arguments:
- activations: bfloat16 [16, 8192, 4096], P('layer', 'tok'), may hold values from -40 to 40, as said below
- sketch: bfloat16 [16, 4096, 512], P('layer'), may hold values from -0.0234375 to 0.0234375
Outputs:
- range_basis: float32 [8, 16, 64, 512], P('tok', 'layer')
- triangle: float32 [512, 512], replicated
- decoder: float32 [512, 16, 4096], P(None, 'layer', 'tok')
The draws below stay inside these ranges and needn't reach their ends.
Inputs may be any that keep to these rules, and one draw needn't show every extreme that they name: `activations`: activations of order one to several, with magnitudes that vary from token to token.
All inputs are finite; a program needn't handle non-finite values.
Results may differ from the reference program's by a relative error of at most 0.0028.
Values may be sent and summed in bfloat16 or wider, within the bound.
A program may use at most 128 MiB of HBM per device.

```python
import math
import jax
import jax.numpy as jnp
from jax import lax

D = 4096
RANK = 512
LAYERS = 16
TOKENS = 8192
N_LAYER = 16
N_TOK = 8


def draw_activations(key, part):
    key = jax.random.fold_in(key, 11)
    noise_key, scale_key = jax.random.split(key, 2)
    noise = jax.random.truncated_normal(noise_key, -4.0, 4.0, (LAYERS, TOKENS, D)).astype(jnp.float32)
    spread = jax.random.uniform(scale_key, (TOKENS,), jnp.float32, 0.0, 1.0)
    position = jnp.arange(TOKENS, dtype=jnp.float32) / TOKENS
    row_scale = 0.3 * jnp.exp(spread * 2.302585) * jnp.exp(position * 1.098612)
    return (noise * row_scale[None, :, None]).astype(jnp.bfloat16)


def block_levels(rng, extent, shards, low, top_value):
    loudness = 1.0
    for dim, blocks in shards:
        draws = jax.random.uniform(jax.random.fold_in(jax.random.fold_in(rng, 6), dim), (blocks,), jnp.float32, low / len(shards), top_value / len(shards))
        loudness = loudness * jnp.repeat(jnp.exp(draws), extent[dim] // blocks).reshape((-1,) + (1,) * (len(extent) - 1 - dim))
    return loudness


def normal_values(rng, extent, deviation, limit, cuts=(), kind=jnp.bfloat16):
    result = jax.random.normal(rng, extent, jnp.float32) * deviation
    if len(cuts) > 0:
        result = block_levels(rng, extent, cuts, -0.22, 0.18) * result
    return jnp.clip(result, min=-limit, max=limit).astype(kind)


def setup_inputs(seed: int = 0) -> dict:
    streams_of = jax.random.split(jax.random.key(seed), 3)
    return {
        "activations": draw_activations(jax.random.fold_in(streams_of[2], 71), 0),
        "sketch": normal_values(streams_of[1], (LAYERS, D, RANK), (LAYERS * D) ** -0.5, 0.0234375, ((0, 16),)),
    }


def reference(activations, sketch):
    sample = jnp.zeros((TOKENS, RANK), jnp.float32)
    for layer_index in range(LAYERS):
        sample = sample + jnp.dot(activations[layer_index].astype(jnp.float32), sketch[layer_index].astype(jnp.float32), preferred_element_type=jnp.float32)
    gram_matrix = jnp.dot(sample.T.astype(jnp.float32), sample.astype(jnp.float32), precision=lax.Precision.HIGHEST, preferred_element_type=jnp.float32) / TOKENS
    cholesky_factor = jnp.linalg.cholesky(gram_matrix)
    triangle = cholesky_factor.T
    basis_full = jax.scipy.linalg.solve_triangular(cholesky_factor, sample.T, lower=True).T
    range_basis = basis_full.reshape(N_TOK, N_LAYER, TOKENS // (N_TOK * N_LAYER), RANK)
    narrow = basis_full.astype(jnp.bfloat16)
    normaliser = 1.0 / math.sqrt(TOKENS)
    layer_blocks = []
    for layer_index in range(LAYERS):
        summed = jnp.dot(narrow.T.astype(jnp.float32), activations[layer_index].astype(jnp.float32), preferred_element_type=jnp.float32)
        layer_blocks.append(summed * normaliser)
    decoder = jnp.stack(layer_blocks, axis=1)
    return (range_basis, triangle, decoder)
```

```python
import math

import jax
import jax.numpy as jnp
from jax import lax
from jax.experimental import pallas as pl
from jax.experimental.pallas import tpu as pltpu
from jax.sharding import PartitionSpec as P

HIGHEST = lax.Precision.HIGHEST
MESH = pl.DeviceIdType.MESH
F32 = jnp.float32
BF16 = jnp.bfloat16
SIDE = 4
HALF = 256


def dot_exact(a, b, ca, cb):
    dims = (((ca,), (cb,)), ((), ()))
    return lax.dot_general(a, b, dims, precision=HIGHEST, preferred_element_type=F32)


def row_of(value, index):
    return jnp.broadcast_to(value[index : index + 1, :], value.shape)


def col_of(value, index):
    return jnp.broadcast_to(value[:, index : index + 1], value.shape)


def eliminate(block):
    size = block.shape[0]
    count = size // 8
    rows = [block[8 * i : 8 * i + 8, :] for i in range(count)]
    sub = lax.broadcasted_iota(jnp.int32, (8, size), 0)
    lane = lax.broadcasted_iota(jnp.int32, (8, size), 1)
    reduced, pivots = [], []
    for b in range(count):
        x = rows[b]
        cols = [col_of(x, 8 * b + k) for k in range(8)]
        u = jnp.zeros_like(x)
        recips = jnp.zeros_like(x)
        pivot_rows = jnp.zeros_like(x)
        for s in range(8):
            at = lane == 8 * b + s
            here = sub == s
            pivot = row_of(cols[s], s)
            recip = 1.0 / pivot
            others = jnp.where(here, 0.0, cols[s])
            row = row_of(x, s)
            u = jnp.where(here, row, u)
            pivot_rows = jnp.where(here, pivot, pivot_rows)
            recips = jnp.where(here, recip, recips)
            row = jnp.where(at, 1.0, row)
            x = jnp.where(at, jnp.where(here, 1.0, 0.0), x) - (others * row) * recip
            for k in range(s + 1, 8):
                cols[k] = cols[k] - (others * row_of(cols[k], s)) * recip
        reduced.append(u)
        pivots.append(pivot_rows)
        if b + 1 < count:
            solved = x * recips
            solved_rows = [row_of(solved, k) for k in range(8)]
            inside = (lane >= 8 * b) & (lane < 8 * b + 8)
            for i in range(b + 1, count):
                y = rows[i]
                t = [col_of(y, 8 * b + k) * solved_rows[k] for k in range(8)]
                t = ((t[0] + t[1]) + (t[2] + t[3])) + ((t[4] + t[5]) + (t[6] + t[7]))
                rows[i] = jnp.where(inside, 0.0, y) - t
    return jnp.concatenate(reduced, 0), jnp.concatenate(pivots, 0)


def factor_block(block):
    reduced, pivots = eliminate(block)
    row = lax.broadcasted_iota(jnp.int32, reduced.shape, 0)
    lane = lax.broadcasted_iota(jnp.int32, reduced.shape, 1)
    scale = lax.rsqrt(pivots)
    upper = jnp.where(lane >= row, reduced, 0.0) * scale
    inverse = jnp.where(lane < row, reduced, jnp.where(lane == row, 1.0, 0.0)) * scale
    return upper, inverse


def cholesky_panel(gram, upper, inverse, start, width):
    size = gram.shape[0]
    stop = start + width
    own = slice(start, stop)
    r, w = factor_block(gram[own, own])
    upper[own, own] = r
    inverse[own, own] = w
    if stop < size:
        rest = slice(stop, size)
        r_rest = dot_exact(w, gram[own, rest], 1, 0)
        upper[own, rest] = r_rest
        upper[rest, own] = jnp.zeros((size - stop, width), F32)
        inverse[own, rest] = jnp.zeros((width, size - stop), F32)
        gram[rest, rest] = gram[rest, rest] - dot_exact(r_rest, r_rest, 0, 0)
    if start:
        before = slice(0, start)
        t = dot_exact(upper[before, own], inverse[before, before], 0, 0)
        inverse[own, before] = -dot_exact(w, t, 1, 0)


def kernel(
    a_hbm, k_hbm,
    q_out, r_out, d_out,
    a, k, part, rx1, rx2, rz1, rz2, px, pz, sg, hi, lo,
    gb, gc, gy, gram, inv,
    away, home, pair, fwd, near,
    load_sem, send_sem, recv_sem,
):
    layer, tok = lax.axis_index("layer"), lax.axis_index("tok")
    z, x = lax.div(layer, SIDE), lax.rem(layer, SIDE)
    y, c = lax.div(tok, 2), lax.rem(tok, 2)
    total_rows = 8 * part.shape[0] * part.shape[1] * part.shape[2]

    def plus(value, step):
        return lax.rem(value + (step + SIDE), SIDE)

    def at_z(step):
        return (plus(z, step) * SIDE + x, tok)

    def at_x(step):
        return (z * SIDE + plus(x, step), tok)

    def at_y(step):
        return (layer, plus(y, step) * 2 + c)

    other_core = (layer, y * 2 + (1 - c))

    used = [0]
    sent, gram_sent = [], []

    def slots(count):
        first = used[0]
        used[0] += count
        return first

    def copy(src, dst, slot, device):
        return pltpu.make_async_remote_copy(
            src_ref=src, dst_ref=dst, send_sem=send_sem.at[slot], recv_sem=recv_sem.at[slot],
            device_id=device, device_id_type=MESH,
        )

    def put(src, dst, slot, device, log=sent):
        sending = copy(src, dst, slot, device)
        sending.start()
        log.append(sending)

    def take(dst, slot, device):
        copy(dst, dst, slot, device).wait_recv()

    barrier = pltpu.get_barrier_semaphore()
    friends = [at_z(s) for s in (1, 2, 3)] + [at_x(s) for s in (1, 2, 3)] + [at_y(s) for s in (1, 2, 3)] + [other_core]
    for friend in friends:
        pl.semaphore_signal(barrier, inc=1, device_id=friend, device_id_type=MESH)

    rows = a.shape[0] // SIDE
    k_load = pltpu.make_async_copy(k_hbm.at[0], k, load_sem.at[SIDE])
    k_load.start()
    chunk_z = [plus(z, i) for i in (1, 2, 3, 0)]
    loads = []
    for i, cz in enumerate(chunk_z):
        span = pl.ds(pl.multiple_of(cz * rows, rows), rows)
        loads.append(pltpu.make_async_copy(a_hbm.at[0, span, :], a.at[span, :], load_sem.at[i]))
        loads[-1].start()
    k_load.wait()

    low, high = pl.ds(0, HALF), pl.ds(HALF, HALF)
    x1, z1, x2, z2 = slots(12), slots(3), slots(3), slots(3)
    for i, cz in enumerate(chunk_z):
        loads[i].wait()
        span = pl.ds(pl.multiple_of(cz * rows, rows), rows)

        @pl.loop(0, 2)
        def _(h):
            cols = pl.ds(pl.multiple_of(h * HALF, HALF), HALF)
            terms = jnp.dot(a[span, :], k[:, cols], preferred_element_type=F32)
            part[cz, :, :, cols] = terms.reshape(part.shape[1], part.shape[2], HALF)

        if i == 0:
            pl.semaphore_wait(barrier, len(friends))
        for s in (1, 2, 3):
            put(part.at[cz, plus(x, s), :, low], rx1.at[s - 1, cz], x1 + 4 * (s - 1) + i, at_x(s))
        if i < 3:
            put(part.at[cz, :, :, high], rz1.at[i], z1 + i, at_z(i + 1))

    for i, cz in enumerate(chunk_z):
        for s in (1, 2, 3):
            take(rx1.at[s - 1, cz], x1 + 4 * (s - 1) + i, at_x(-s))
        px[cz] = (part[cz, x, :, low] + rx1[0, cz]) + (rx1[1, cz] + rx1[2, cz])
        if i < 3:
            put(px.at[cz], rx2.at[i], x2 + i, at_z(i + 1))
    for s in (1, 2, 3):
        take(rz1.at[s - 1], z1 + s - 1, at_z(-s))
    pz[...] = (part[z, :, :, high] + rz1[0]) + (rz1[1] + rz1[2])
    for s in (1, 2, 3):
        put(pz.at[plus(x, s)], rz2.at[s - 1], z2 + s - 1, at_x(s))
    for s in (1, 2, 3):
        take(rx2.at[s - 1], x2 + s - 1, at_z(-s))
    sg[z, x, :, low] = (px[z] + rx2[0]) + (rx2[1] + rx2[2])

    xa, xb, za, zb = slots(3), slots(12), slots(3), slots(12)
    for s in (1, 2, 3):
        put(sg.at[z, x, :, low], sg.at[z, x, :, low], xa + s - 1, at_z(s))
    for s in (1, 2, 3):
        put(sg.at[z, x, :, low], sg.at[z, x, :, low], xb + s - 1, at_x(s))
    for s in (1, 2, 3):
        take(rz2.at[s - 1], z2 + s - 1, at_x(-s))
    sg[z, x, :, high] = (pz[x] + rz2[0]) + (rz2[1] + rz2[2])
    for s in (1, 2, 3):
        put(sg.at[z, x, :, high], sg.at[z, x, :, high], za + s - 1, at_x(s))
    for s in (1, 2, 3):
        put(sg.at[z, x, :, high], sg.at[z, x, :, high], zb + s - 1, at_z(s))
    for m in (1, 2, 3):
        mz, mx = plus(z, -m), plus(x, -m)
        take(sg.at[mz, x, :, low], xa + m - 1, at_z(-m))
        for s in (1, 2, 3):
            put(sg.at[mz, x, :, low], sg.at[mz, x, :, low], xb + 3 * m + s - 1, at_x(s))
        take(sg.at[z, mx, :, high], za + m - 1, at_x(-m))
        for s in (1, 2, 3):
            put(sg.at[z, mx, :, high], sg.at[z, mx, :, high], zb + 3 * m + s - 1, at_z(s))
    for m in range(4):
        mz, mx = plus(z, -m), plus(x, -m)
        for s in (1, 2, 3):
            take(sg.at[mz, plus(x, -s), :, low], xb + 3 * m + s - 1, at_x(-s))
            take(sg.at[plus(z, -s), mx, :, high], zb + 3 * m + s - 1, at_z(-s))

    wide = 128
    block_rows = pl.ds(pl.multiple_of(z * wide, wide), wide)
    block_cols = pl.ds(pl.multiple_of(x * wide, wide), wide)
    group = part.shape[0] * part.shape[1] * part.shape[2]
    left = sg[:, :, :, block_rows].reshape(group, wide)
    right = sg[:, :, :, block_cols].reshape(group, wide)
    gb[...] = dot_exact(left, right, 0, 0).reshape(2, wide // 2, wide) * (1.0 / total_rows)
    g_core = slots(1)
    put(gb.at[1 - c], gc, g_core, other_core)

    @pl.loop(0, SIDE)
    def _(i):
        value = sg[i].reshape(group // SIDE, sg.shape[3]).T
        top = value.astype(BF16)
        cols = pl.ds(pl.multiple_of(i * (group // SIDE), group // SIDE), group // SIDE)
        hi[:, cols] = top
        lo[:, cols] = (value - top.astype(F32)).astype(BF16)

    width = d_out.shape[1]

    def project(dst, step, core):
        owner = plus(y, step) * 2 + core

        @pl.loop(0, width // HALF)
        def _(h):
            cols = pl.ds(pl.multiple_of(owner * width + h * HALF, HALF), HALF)
            block = a[:, cols]
            value = jnp.dot(hi[...], block, preferred_element_type=F32)
            value = value + jnp.dot(lo[...], block, preferred_element_type=F32)
            dst[:, pl.ds(pl.multiple_of(h * HALF, HALF), HALF)] = value

    p_core = slots(4)
    order = (2, 1, 3, 0)

    def project_both(i):
        project(away.at[i], order[i], 1 - c)
        put(away.at[i], pair.at[i], p_core + i, other_core)
        project(home.at[i], order[i], c)

    def add_pair(i):
        take(pair.at[i], p_core + i, other_core)
        home[i] = home[i] + pair[i]

    top, bottom = pl.ds(0, HALF), pl.ds(HALF, HALF)
    f_up, f_down, n_up, n_down = slots(1), slots(1), slots(2), slots(2)
    g_y, ga, gbx, gaz, gbz, g_swap = slots(3), slots(3), slots(12), slots(3), slots(12), slots(1)

    project_both(0)
    take(gc, g_core, other_core)
    gy[y] = gb[c] + gc[...]
    for s in (1, 2, 3):
        put(gy.at[y], gy.at[y], g_y + s - 1, at_y(s))
    project_both(1)
    add_pair(0)
    put(home.at[0, top, :], fwd.at[0], f_up, at_y(1))
    put(home.at[0, bottom, :], fwd.at[1], f_down, at_y(-1))

    def piece(pz_, px_, part_index):
        r = pl.ds(pl.multiple_of(pz_ * wide + c * (wide // 2) + part_index * (wide // 4), wide // 4), wide // 4)
        return gram.at[r, pl.ds(pl.multiple_of(px_ * wide, wide), wide)]

    for s in (1, 2, 3):
        take(gy.at[plus(y, -s)], g_y + s - 1, at_y(-s))
    mine = pl.ds(pl.multiple_of(z * wide + c * (wide // 2), wide // 2), wide // 2)
    gram[mine, block_cols] = (gy[0] + gy[1]) + (gy[2] + gy[3])
    for s in (1, 2, 3):
        put(piece(z, x, 0), piece(z, x, 0), ga + s - 1, at_z(s), gram_sent)
        put(piece(z, x, 1), piece(z, x, 1), gaz + s - 1, at_x(s), gram_sent)
    for s in (1, 2, 3):
        put(piece(z, x, 0), piece(z, x, 0), gbx + s - 1, at_x(s), gram_sent)
        put(piece(z, x, 1), piece(z, x, 1), gbz + s - 1, at_z(s), gram_sent)
    project_both(2)
    for m in (1, 2, 3):
        mz, mx = plus(z, -m), plus(x, -m)
        take(piece(mz, x, 0), ga + m - 1, at_z(-m))
        for s in (1, 2, 3):
            put(piece(mz, x, 0), piece(mz, x, 0), gbx + 3 * m + s - 1, at_x(s), gram_sent)
        take(piece(z, mx, 1), gaz + m - 1, at_x(-m))
        for s in (1, 2, 3):
            put(piece(z, mx, 1), piece(z, mx, 1), gbz + 3 * m + s - 1, at_z(s), gram_sent)
    add_pair(1)
    put(home.at[1, bottom, :], near.at[0, bottom, :], n_up, at_y(1))
    project_both(3)
    for m in range(4):
        mz, mx = plus(z, -m), plus(x, -m)
        for s in (1, 2, 3):
            take(piece(mz, plus(x, -s), 0), gbx + 3 * m + s - 1, at_x(-s))
            take(piece(plus(z, -s), mx, 1), gbz + 3 * m + s - 1, at_z(-s))
    for i in range(SIDE):
        rows_here = pl.ds(pl.multiple_of(i * wide + c * (wide // 2), wide // 2), wide // 2)
        if i == 0:
            g_swaps = slots(SIDE)
        put(gram.at[rows_here, :], gram.at[rows_here, :], g_swaps + i, other_core, gram_sent)
    add_pair(2)
    put(home.at[2, top, :], near.at[1, top, :], n_down, at_y(-1))
    add_pair(3)
    for i in range(SIDE):
        rows_there = pl.ds(pl.multiple_of(i * wide + (1 - c) * (wide // 2), wide // 2), wide // 2)
        take(gram.at[rows_there, :], g_swaps + i, other_core)

    for sending in gram_sent:
        sending.wait_send()
    cholesky_panel(gram, r_out, inv, 0, wide)
    take(fwd.at[0], f_up, at_y(-1))
    home[1, top, :] = home[1, top, :] + fwd[0]
    put(home.at[1, top, :], near.at[0, top, :], n_up + 1, at_y(1))
    take(fwd.at[1], f_down, at_y(1))
    home[2, bottom, :] = home[2, bottom, :] + fwd[1]
    put(home.at[2, bottom, :], near.at[1, bottom, :], n_down + 1, at_y(-1))
    for start in range(wide, gram.shape[0], wide):
        cholesky_panel(gram, r_out, inv, start, wide)

    own = sg[z, x]
    q_out[...] = dot_exact(own, inv[...], 1, 1)
    take(near.at[0, bottom, :], n_up, at_y(-1))
    take(near.at[1, top, :], n_down, at_y(1))
    take(near.at[0, top, :], n_up + 1, at_y(-1))
    take(near.at[1, bottom, :], n_down + 1, at_y(1))
    scale = 1.0 / math.sqrt(total_rows)

    @pl.loop(0, width // HALF)
    def _(h):
        cols = pl.ds(pl.multiple_of(h * HALF, HALF), HALF)
        total = (home[3, :, cols] + near[0, :, cols]) + near[1, :, cols]
        d_out[:, cols] = dot_exact(inv[...], total * scale, 1, 0)

    for sending in sent:
        sending.wait_send()


def on_device(activations, sketch):
    _, rows, depth = activations.shape
    rank = sketch.shape[2]
    strip = rows // 16
    width = depth // 8
    vmem = pltpu.VMEM
    q, r, d = pl.pallas_call(
        kernel,
        out_shape=(
            jax.ShapeDtypeStruct((strip, rank), F32),
            jax.ShapeDtypeStruct((rank, rank), F32),
            jax.ShapeDtypeStruct((rank, width), F32),
        ),
        in_specs=[pl.BlockSpec(memory_space=pl.ANY)] * 2,
        out_specs=(pl.BlockSpec(memory_space=pltpu.VMEM),) * 3,
        scratch_shapes=[
            vmem((rows, depth), BF16),
            vmem((depth, rank), BF16),
            vmem((4, 4, strip, rank), F32),
            vmem((3, 4, strip, HALF), F32),
            vmem((3, strip, HALF), F32),
            vmem((3, 4, strip, HALF), F32),
            vmem((3, strip, HALF), F32),
            vmem((4, strip, HALF), F32),
            vmem((4, strip, HALF), F32),
            vmem((4, 4, strip, rank), F32),
            vmem((rank, rows), BF16),
            vmem((rank, rows), BF16),
            vmem((2, 64, 128), F32),
            vmem((64, 128), F32),
            vmem((4, 64, 128), F32),
            vmem((rank, rank), F32),
            vmem((rank, rank), F32),
            vmem((4, rank, width), F32),
            vmem((4, rank, width), F32),
            vmem((4, rank, width), F32),
            vmem((2, HALF, width), F32),
            vmem((2, rank, width), F32),
            pltpu.SemaphoreType.DMA((5,)),
            pltpu.SemaphoreType.DMA((112,)),
            pltpu.SemaphoreType.DMA((112,)),
        ],
        compiler_params=pltpu.CompilerParams(
            collective_id=0, has_side_effects=True, vmem_limit_bytes=56 << 20
        ),
        cost_estimate=pl.CostEstimate(flops=16 * rows * depth * rank, bytes_accessed=16 << 20, transcendentals=0),
    )(activations, sketch)
    return q.reshape(1, 1, strip, rank), r, d.reshape(rank, 1, width)


def solution(mesh):
    return jax.shard_map(
        on_device,
        mesh=mesh,
        in_specs=(P("layer", "tok", None), P("layer", None, None)),
        out_specs=(P("tok", "layer", None, None), P(), P(None, "layer", "tok")),
        check_vma=False,
    )
```
